256 devices in a mesh: rows: 64 (over x, z_hi, y), rep: 4 (over z_lo, core).
Axes of the slice: x: 4, y: 4, z: 8 (z_hi: 4, z_lo: 2; z = z_hi * 2 + z_lo), core: 2. Of those that a mesh axis runs over, the one named last changes fastest.
Arguments:
- features: float32 [32768, 256], P(('rows', 'rep')), may hold values from -6 to 6
- weight: float32 [256, 256], replicated, may hold values from -0.375 to 0.375
- cotangent: float32 [32768, 256], P(('rows', 'rep')), may hold values from -6 to 6
- tiles: float32 [64, 4, 64, 2, 128, 128], P('rows', 'rep'), may hold values from -0.046875 to 0.046875
- tile_count: int32 [64, 4, 64], P('rows', 'rep'), may hold values from 0 to 2, as said below
- tile_block: int32 [64, 4, 64, 2], P('rows', 'rep'), may hold values from 0 to 3, as said below
Outputs:
- hidden: float32 [32768, 256], P(('rows', 'rep'))
- grad_weight: float32 [256, 256], replicated
- grad_features: float32 [32768, 256], P(('rows', 'rep'))
The draws below stay inside these ranges and needn't reach their ends.
Inputs may be any that keep to these rules, and one draw needn't show every extreme that they name: `tile_count`: at the section equal to the row group, every column block holds 2 live tiles. `tile_block`: the blocks named by one section's slots are distinct; slots at or beyond the section's count are ignored.
All inputs are finite; a program needn't handle non-finite values.
Results may differ from the reference program's by a relative error of at most 0.0001.
Values sent between devices are 32-bit elements; how exact they have to be, the bound alone decides.
No kernel may reach another device: no remote copies, remote signals or barrier semaphores. Data moves between devices by JAX's collectives and lax.ppermute only.
A program may use at most 128 MiB of HBM per device.

```python
import math
import jax
import jax.numpy as jnp
from jax import lax

F = 256
BLK = 128
TPS = 2
NODES = 32768
N_ROWS = 64
N_REP = 4


def draw_tile_count(key, part):
    key = jax.random.fold_in(key, 11)
    first_key, second_key = jax.random.split(key)
    level = jax.random.randint(first_key, (N_ROWS, 1, 1), 1, 2 * TPS + 1)
    raw = jax.random.randint(second_key, (N_ROWS, N_REP, N_ROWS), 0, level + 1)
    count = jnp.minimum(raw, TPS)
    own = jnp.arange(N_ROWS)[:, None, None] == jnp.arange(N_ROWS)[None, None, :]
    return jnp.where(own, TPS, count).astype(jnp.int32)


def draw_tile_block(key, part):
    key = jax.random.fold_in(key, 23)
    scores = jax.random.randint(key, (N_ROWS, N_REP, N_ROWS, N_REP), 0, 1 << 20) * N_REP + jnp.arange(N_REP)
    order = jnp.argsort(scores, axis=-1, stable=True)[..., :TPS]
    return order.astype(jnp.int32)


def block_levels(rng, extent, shards, smallest, largest):
    factor_of, own = 1.0, jax.random.fold_in(rng, 6)
    for axis_at, blocks in shards:
        steps = jnp.exp(jax.random.uniform(jax.random.fold_in(own, axis_at), (blocks,), jnp.float32, smallest / len(shards), largest / len(shards)))
        factor_of = factor_of * jnp.repeat(steps, extent[axis_at] // blocks).reshape([-1 if axis == axis_at else 1 for axis in range(len(extent))])
    return factor_of


def bell_draw(stream_key, extent, width, reach, pieces=(), held_as=jnp.bfloat16):
    factor_of = block_levels(stream_key, extent, pieces, -0.22, 0.18) if pieces else 1.0
    values = jax.random.normal(stream_key, extent, jnp.float32) * width * factor_of
    return jnp.minimum(jnp.maximum(values, -reach), reach).astype(held_as)


def setup_inputs(seed: int = 0) -> dict:
    key_of = jax.random.split(jax.random.key(seed), 7)
    return {
        "features": bell_draw(key_of[0], (NODES, F), 1.0, 6.0, ((0, 256),), jnp.float32),
        "weight": bell_draw(key_of[1], (F, F), F ** -0.5, 0.375, (), jnp.float32),
        "cotangent": bell_draw(key_of[2], (NODES, F), 1.0, 6.0, ((0, 256),), jnp.float32),
        "tiles": bell_draw(key_of[3], (N_ROWS, N_REP, N_ROWS, TPS, BLK, BLK), (BLK * N_ROWS * 2) ** -0.5, 0.046875, ((0, 64), (1, 4)), jnp.float32),
        "tile_count": draw_tile_count(jax.random.fold_in(key_of[6], 71), 0),
        "tile_block": draw_tile_block(jax.random.fold_in(key_of[6], 71), 0),
    }


def silu_slope(pre):
    sig = jax.nn.sigmoid(pre)
    return sig * (1.0 + pre * (1.0 - sig))

def reference(features, weight, cotangent, tiles, tile_count, tile_block):
    highest = lax.Precision.HIGHEST
    blocks = jnp.arange(N_REP, dtype=jnp.int32)
    slots = jnp.arange(TPS, dtype=jnp.int32)
    select = ((tile_block[..., None] == blocks) & (slots[:, None] < tile_count[..., None, None])).astype(jnp.float32)
    panels = features.reshape(N_ROWS, N_REP, BLK, F)

    def forward_group(pair):
        group_tiles, group_select = pair
        prods = jnp.einsum('rstab,srbf->rstaf', group_tiles, panels, precision=highest)
        return jnp.einsum('rstk,rstaf->kaf', group_select, prods, precision=highest)
    aggregated = lax.map(forward_group, (tiles, select)).reshape(NODES, F)
    pre = jnp.dot(aggregated, weight, precision=highest)
    hidden = jax.nn.silu(pre)
    delta = cotangent * silu_slope(pre)
    grad_weight = jnp.dot(aggregated.T, delta, precision=highest) / math.sqrt(NODES)
    back = jnp.dot(delta, weight.T, precision=highest).reshape(N_ROWS, N_REP, BLK, F)

    def backward_group(carry, triple):
        group_tiles, group_select, group_back = triple
        picked = jnp.einsum('rstk,kaf->rstaf', group_select, group_back, precision=highest)
        return (carry + jnp.einsum('rstab,rstaf->srbf', group_tiles, picked, precision=highest), None)
    start_grad = jnp.zeros((N_ROWS, N_REP, BLK, F), jnp.float32)
    grad_features, _ = lax.scan(backward_group, start_grad, (tiles, select, back))
    return (hidden, grad_weight, grad_features.reshape(NODES, F))
```

```python
import functools
import math

import jax
import jax.numpy as jnp
from jax import lax
from jax.experimental import pallas as pl
from jax.experimental.pallas import tpu as pltpu
from jax.sharding import PartitionSpec as P

SIDE = 4
F32 = jnp.float32
BF16 = jnp.bfloat16


def row_index(x, z, y):
    return (x * SIDE + z) * SIDE + y


def toward(axis, step):
    pairs = []
    for x in range(SIDE):
        for z in range(SIDE):
            for y in range(SIDE):
                at = [x, z, y]
                at["xzy".index(axis)] = (at["xzy".index(axis)] + step) % SIDE
                pairs.append((row_index(x, z, y), row_index(*at)))
    return pairs


def send(value, axis, step):
    return lax.ppermute(value, "rows", toward(axis, step))


def swap(value, bit):
    return lax.ppermute(value, "rep", [(r, r ^ bit) for r in range(4)])


def split(value):
    high = value.astype(BF16)
    return high, (value - high.astype(F32)).astype(BF16)


def mm(left, right):
    return jnp.dot(left, right, preferred_element_type=F32)


def panel_kernel(at_ref, count_ref, block_ref, tiles_ref, high_ref, low_ref):
    x = lax.rem(at_ref[0] + pl.program_id(0), SIDE)
    z = lax.rem(at_ref[1] + pl.program_id(1), SIDE)
    for dy in range(SIDE):
        y = lax.rem(at_ref[2] + dy, SIDE)
        section = row_index(x, z, y)
        count = count_ref[section]
        first, second = block_ref[2 * section], block_ref[2 * section + 1]
        for k in range(4):
            w0 = jnp.where((first == k) & (count > 0), 1.0, 0.0).astype(F32)
            w1 = jnp.where((second == k) & (count > 1), 1.0, 0.0).astype(F32)
            high, low = split(tiles_ref[0, 0, y, 0] * w0 + tiles_ref[0, 0, y, 1] * w1)
            high_ref[0, dy, 0, pl.ds(k * 128, 128), :] = high
            low_ref[0, dy, 0, pl.ds(k * 128, 128), :] = low


def make_panel(at, counts, blocks, tiles):
    shape = jax.ShapeDtypeStruct((SIDE, SIDE, SIDE, 512, 128), BF16)
    out_spec = pl.BlockSpec((1, SIDE, 1, 512, 128), lambda i, j, at, c, b: (i, 0, j, 0, 0))
    return pl.pallas_call(
        panel_kernel,
        grid_spec=pltpu.PrefetchScalarGridSpec(
            num_scalar_prefetch=3,
            grid=(SIDE, SIDE),
            in_specs=[
                pl.BlockSpec(
                    (1, 1, SIDE, 2, 128, 128),
                    lambda i, j, at, c, b: (
                        lax.rem(at[0] + i, SIDE),
                        lax.rem(at[1] + j, SIDE),
                        0,
                        0,
                        0,
                        0,
                    ),
                )
            ],
            out_specs=[out_spec, out_spec],
        ),
        out_shape=[shape, shape],
        cost_estimate=pl.CostEstimate(flops=10**8, bytes_accessed=25 * 10**6, transcendentals=0),
        compiler_params=pltpu.CompilerParams(vmem_limit_bytes=32 * 2**20),
        name="panel",
    )(at, counts, blocks, tiles.reshape(SIDE, SIDE, SIDE, 2, 128, 128))


def panel_spec(half, pick):
    def index(i):
        d, o = pick(i)
        return (d, o, 0, 0, 0) if half == 0 else (o, d, 0, 0, 0)

    return pl.BlockSpec((1, 1, SIDE, 512, 128), index)


def wide(ref):
    return jnp.concatenate([ref[0, 0, dz] for dz in range(SIDE)], axis=1)


def forward_kernel(halves, *refs):
    n = len(halves)
    highs, lows, blocks = refs[:n], refs[n : 2 * n], refs[2 * n : 3 * n]
    starts, totals = refs[3 * n : 3 * n + 2], refs[3 * n + 2 :]

    @pl.when(pl.program_id(0) == 0)
    def _():
        for start, total in zip(starts, totals):
            total[...] = start[...]

    for half, high, low, block in zip(halves, highs, lows, blocks):
        g_high, g_low = split(block[0].reshape(SIDE * 128, 128))
        both = mm(wide(high), jnp.concatenate([g_high, g_low], axis=1))
        totals[half][...] += both[:, :128] + (both[:, 128:] + mm(wide(low), g_high))


def forward(panel, totals, steps, jobs):
    whole = pl.BlockSpec((512, 128), lambda i: (0, 0))
    specs = [panel_spec(half, pick) for half, pick, _ in jobs]
    return pl.pallas_call(
        functools.partial(forward_kernel, [half for half, _, _ in jobs]),
        grid=(steps,),
        in_specs=specs
        + specs
        + [pl.BlockSpec((1, SIDE, 128, 128), lambda i: (i, 0, 0, 0)) for _ in jobs]
        + [whole, whole],
        out_specs=[whole, whole],
        out_shape=[jax.ShapeDtypeStruct((512, 128), F32)] * 2,
        cost_estimate=pl.CostEstimate(
            flops=len(jobs) * steps * 4 * 2 * 512 * 512 * 128,
            bytes_accessed=len(jobs) * steps * 13 * 10**5,
            transcendentals=0,
        ),
        compiler_params=pltpu.CompilerParams(vmem_limit_bytes=48 * 2**20),
        name="forward",
    )(*[panel[0]] * len(jobs), *[panel[1]] * len(jobs), *[array for _, _, array in jobs], *totals)


def middle_kernel(own_ref, other_ref, weight_ref, cot_ref, hidden_ref, term_ref, back_ref):
    highest = lax.Precision.HIGHEST
    aggregated = own_ref[...] + other_ref[...]
    weight = weight_ref[...]
    pre = jnp.dot(aggregated, weight, precision=highest, preferred_element_type=F32)
    sig = 1.0 / (1.0 + jnp.exp(-pre))
    hidden_ref[...] = pre * sig
    delta = cot_ref[...] * (sig * (1.0 + pre * (1.0 - sig)))
    back_ref[...] = lax.dot_general(
        weight, delta, (((1,), (1,)), ((), ())), precision=highest, preferred_element_type=F32
    )
    term_ref[...] = jnp.dot(aggregated.T, delta, precision=highest, preferred_element_type=F32)


def middle(own, other, weight, cotangent):
    return pl.pallas_call(
        middle_kernel,
        out_shape=[
            jax.ShapeDtypeStruct((128, 256), F32),
            jax.ShapeDtypeStruct((256, 256), F32),
            jax.ShapeDtypeStruct((256, 128), F32),
        ],
        compiler_params=pltpu.CompilerParams(vmem_limit_bytes=32 * 2**20),
        name="middle",
    )(own, other, weight, cotangent)


def backward_kernel(halves, back_ref, *refs):
    n = len(halves)
    highs, lows, outs = refs[:n], refs[n : 2 * n], refs[2 * n :]
    for half, high, low, out in zip(halves, highs, lows, outs):
        back = jnp.concatenate([back_ref[k, pl.ds(half * 128, 128), :] for k in range(4)], axis=1)
        b_high, b_low = split(back)
        both = mm(jnp.concatenate([b_high, b_low], axis=0), wide(high))
        result = both[:128] + (both[128:] + mm(b_high, wide(low)))
        for dz in range(SIDE):
            out[0, dz] = result[:, dz * 128 : (dz + 1) * 128]


def backward(panel, back, steps, jobs):
    specs = [panel_spec(half, pick) for half, pick in jobs]
    return pl.pallas_call(
        functools.partial(backward_kernel, [half for half, _ in jobs]),
        grid=(steps,),
        in_specs=[pl.BlockSpec((4, 256, 128), lambda i: (0, 0, 0))] + specs + specs,
        out_specs=[pl.BlockSpec((1, SIDE, 128, 128), lambda i: (i, 0, 0, 0)) for _ in jobs],
        out_shape=[jax.ShapeDtypeStruct((steps, SIDE, 128, 128), F32) for _ in jobs],
        cost_estimate=pl.CostEstimate(
            flops=len(jobs) * steps * 4 * 2 * 512 * 512 * 128,
            bytes_accessed=len(jobs) * steps * 13 * 10**5,
            transcendentals=0,
        ),
        compiler_params=pltpu.CompilerParams(vmem_limit_bytes=48 * 2**20),
        name="backward",
    )(back, *[panel[0]] * len(jobs), *[panel[1]] * len(jobs))


BIG = ("x", "y")
MID = ("y", "x")


def gather_forward(features, panel):
    two = jnp.stack([features[:, :128], features[:, 128:]])
    by_z = [two] + [send(two, "z", -d) for d in (1, 2, 3)]
    totals = [jnp.zeros((512, 128), F32)] * 2
    near = []
    for half in range(2):
        mine = jnp.stack([block[half] for block in by_z])
        near.append(jnp.stack([mine] + [send(mine, MID[half], -d) for d in (1, 2, 3)]))
    first = [(send(near[h], BIG[h], -1), send(near[h], BIG[h], 1)) for h in range(2)]
    second = [
        (send(first[h][0][:2], BIG[h], -1), send(first[h][1][2:], BIG[h], 1)) for h in range(2)
    ]
    totals = forward(panel, totals, 4, [(h, lambda i: (0, i), near[h]) for h in range(2)])
    totals = forward(
        panel,
        totals,
        4,
        [(h, lambda i, d=d: (d, i), first[h][j]) for h in range(2) for j, d in enumerate((1, 3))],
    )
    return forward(
        panel,
        totals,
        2,
        [(h, lambda i, j=j: (2, 2 * j + i), second[h][j]) for h in range(2) for j in range(2)],
    )


def scatter_backward(back, panel):
    early = backward(
        panel,
        back,
        4,
        [
            (h, pick)
            for h in range(2)
            for pick in (
                lambda i: (1 + i // 2, (i + 2) % 4),
                lambda i: (3 - i // 2, i),
            )
        ],
    )
    late = backward(
        panel,
        back,
        2,
        [
            (h, pick)
            for h in range(2)
            for pick in (
                lambda i: (1, i),
                lambda i: (3, i + 2),
                lambda i: (0, i),
                lambda i: (0, i + 2),
            )
        ],
    )
    by_half = []
    for h in range(2):
        up, down = early[2 * h], early[2 * h + 1]
        late_up, late_down, own_a, own_b = late[4 * h : 4 * h + 4]
        from_below, from_above = send(up, BIG[h], 1), send(down, BIG[h], -1)
        relay_up = send(late_up + from_below[2:], BIG[h], 1)
        relay_down = send(late_down + from_above[2:], BIG[h], -1)
        part_a = own_a + from_above[:2] + relay_up
        part_b = own_b + from_below[:2] + relay_down
        by_half.append(
            part_a[0]
            + send(part_a[1], MID[h], 1)
            + send(part_b[0], MID[h], 2)
            + send(part_b[1], MID[h], 3)
        )
    both = jnp.stack(by_half, axis=1)
    total = both[0] + send(both[1], "z", 1) + send(both[2], "z", 2) + send(both[3], "z", 3)
    return total.reshape(256, 128).T


def pick_two(value, r):
    core, low = r % 2, r // 2
    kept = lax.dynamic_index_in_dim(value, core, 1, keepdims=False)
    given = lax.dynamic_index_in_dim(value, 1 - core, 1, keepdims=False)
    pair = kept + swap(given, 1)
    mine = lax.dynamic_index_in_dim(pair, low, 0, keepdims=False)
    return mine, swap(lax.dynamic_index_in_dim(pair, 1 - low, 0, keepdims=False), 2)


def body(features, weight, cotangent, tiles, tile_count, tile_block):
    g, r = lax.axis_index("rows"), lax.axis_index("rep")
    at = jnp.stack([g // 16, (g // 4) % 4, g % 4]).astype(jnp.int32)
    panel = make_panel(at, tile_count.reshape(-1), tile_block.reshape(-1), tiles[0, 0])
    totals = gather_forward(features, panel)
    partial = jnp.concatenate(totals, axis=1).reshape(2, 2, 128, 256)
    own, other = pick_two(partial, r)
    hidden, term, back = middle(own, other, weight, cotangent)
    back = lax.all_gather(back, "rep", axis=0, tiled=False)
    grad_features = scatter_backward(back, panel)
    mine, theirs = pick_two(term.reshape(2, 2, 64, 256), r)
    piece = mine + theirs
    for axis in "zyx":
        piece = (piece + send(piece, axis, 2)) + (send(piece, axis, 1) + send(piece, axis, 3))
    node_total = 128 * lax.axis_size("rows") * lax.axis_size("rep")
    grad_weight = lax.all_gather(piece, "rep", axis=0, tiled=True) / math.sqrt(node_total)
    return hidden, grad_weight, grad_features


def solution(mesh):
    in_specs = (
        P(("rows", "rep"), None),
        P(),
        P(("rows", "rep"), None),
        P("rows", "rep", None, None, None, None),
        P("rows", "rep", None),
        P("rows", "rep", None, None),
    )
    out_specs = (P(("rows", "rep"), None), P(), P(("rows", "rep"), None))
    return jax.shard_map(body, mesh=mesh, in_specs=in_specs, out_specs=out_specs, check_vma=False)
```

```python
import functools
import math

import jax
import jax.numpy as jnp
from jax import lax
from jax.experimental import pallas as pl
from jax.experimental.pallas import tpu as pltpu
from jax.sharding import PartitionSpec as P

SIDE = 4
F32 = jnp.float32
BF16 = jnp.bfloat16
LIMIT = 16 * 2**20


def row_index(x, z, y):
    return (x * SIDE + z) * SIDE + y


def toward(axis, step):
    pairs = []
    for x in range(SIDE):
        for z in range(SIDE):
            for y in range(SIDE):
                at = [x, z, y]
                at["xzy".index(axis)] = (at["xzy".index(axis)] + step) % SIDE
                pairs.append((row_index(x, z, y), row_index(*at)))
    return pairs


def send(value, axis, step):
    return lax.ppermute(value, "rows", toward(axis, step))


def trade(value, axis, mask):
    pairs = []
    for x in range(SIDE):
        for z in range(SIDE):
            for y in range(SIDE):
                at = [x, z, y]
                at["xzy".index(axis)] ^= mask
                pairs.append((row_index(x, z, y), row_index(*at)))
    return lax.ppermute(value, "rows", pairs)


def swap(value, bit):
    return lax.ppermute(value, "rep", [(r, r ^ bit) for r in range(4)])


def split(value):
    high = value.astype(BF16)
    return high, (value - high.astype(F32)).astype(BF16)


def mm(left, right):
    return jnp.dot(left, right, preferred_element_type=F32)


def panel_kernel(at_ref, count_ref, block_ref, tiles_ref, high_ref, low_ref):
    x = lax.rem(at_ref[0] + pl.program_id(0), SIDE)
    z = lax.rem(at_ref[1] + pl.program_id(1), SIDE)
    for dy in range(SIDE):
        y = lax.rem(at_ref[2] + dy, SIDE)
        section = row_index(x, z, y)
        count = count_ref[section]
        first, second = block_ref[2 * section], block_ref[2 * section + 1]
        for k in range(4):
            block = at_ref[3] ^ k
            w0 = jnp.where((first == block) & (count > 0), 1.0, 0.0).astype(F32)
            w1 = jnp.where((second == block) & (count > 1), 1.0, 0.0).astype(F32)
            high, low = split(tiles_ref[0, 0, y, 0] * w0 + tiles_ref[0, 0, y, 1] * w1)
            high_ref[0, dy, 0, pl.ds(k * 128, 128), :] = high
            low_ref[0, dy, 0, pl.ds(k * 128, 128), :] = low


def make_panel(at, counts, blocks, tiles):
    shape = jax.ShapeDtypeStruct((SIDE, SIDE, SIDE, 512, 128), BF16)
    out_spec = pl.BlockSpec((1, SIDE, 1, 512, 128), lambda i, j, at, c, b: (i, 0, j, 0, 0))
    return pl.pallas_call(
        panel_kernel,
        grid_spec=pltpu.PrefetchScalarGridSpec(
            num_scalar_prefetch=3,
            grid=(SIDE, SIDE),
            in_specs=[
                pl.BlockSpec(
                    (1, 1, SIDE, 2, 128, 128),
                    lambda i, j, at, c, b: (
                        lax.rem(at[0] + i, SIDE),
                        lax.rem(at[1] + j, SIDE),
                        0,
                        0,
                        0,
                        0,
                    ),
                )
            ],
            out_specs=[out_spec, out_spec],
        ),
        out_shape=[shape, shape],
        cost_estimate=pl.CostEstimate(flops=10**8, bytes_accessed=25 * 10**6, transcendentals=0),
        compiler_params=pltpu.CompilerParams(vmem_limit_bytes=LIMIT),
        name="panel",
    )(at, counts, blocks, tiles.reshape(SIDE, SIDE, SIDE, 2, 128, 128))


def wide(ref, half, place):
    d, o = place
    i, j = (d, o) if half == 0 else (o, d)
    return jnp.concatenate([ref[i, j, dz] for dz in range(SIDE)], axis=1)


IN_VMEM = pl.BlockSpec(memory_space=pltpu.VMEM)


def forward_kernel(jobs, high, low, *refs):
    n = len(jobs)
    blocks, starts, totals = refs[:n], refs[n : n + 2], refs[n + 2 :]
    i = pl.program_id(0)

    @pl.when(i == 0)
    def _():
        for start, total in zip(starts, totals):
            total[...] = start[...]

    for (half, pick), block in zip(jobs, blocks):
        g_high, g_low = split(block[0].reshape(SIDE * 128, 128))
        both = mm(wide(high, half, pick(i)), jnp.concatenate([g_high, g_low], axis=1))
        totals[half][...] += both[:, :128] + (both[:, 128:] + mm(wide(low, half, pick(i)), g_high))


def forward(panel, totals, steps, jobs):
    whole = pl.BlockSpec((512, 128), lambda i: (0, 0))
    return pl.pallas_call(
        functools.partial(forward_kernel, [job[:2] for job in jobs]),
        grid=(steps,),
        in_specs=[IN_VMEM, IN_VMEM]
        + [pl.BlockSpec((1, SIDE, 128, 128), lambda i: (i, 0, 0, 0)) for _ in jobs]
        + [whole, whole],
        out_specs=[whole, whole],
        out_shape=[jax.ShapeDtypeStruct((512, 128), F32)] * 2,
        cost_estimate=pl.CostEstimate(
            flops=len(jobs) * steps * 4 * 2 * 512 * 512 * 128,
            bytes_accessed=len(jobs) * steps * 13 * 10**5,
            transcendentals=0,
        ),
        compiler_params=pltpu.CompilerParams(vmem_limit_bytes=LIMIT),
        name="forward",
    )(*panel, *[array for _, _, array in jobs], *totals)


def middle_kernel(at_ref, own_ref, other_ref, weight_ref, cot_ref, high, low, hidden_ref, term_ref, back_ref):
    highest = lax.Precision.HIGHEST
    aggregated = own_ref[...] + other_ref[...]
    weight = weight_ref[...]
    pre = jnp.dot(aggregated, weight, precision=highest, preferred_element_type=F32)
    sig = 1.0 / (1.0 + jnp.exp(-pre))
    hidden_ref[...] = pre * sig
    delta = cot_ref[...] * (sig * (1.0 + pre * (1.0 - sig)))
    back_ref[...] = lax.dot_general(
        weight, delta, (((1,), (1,)), ((), ())), precision=highest, preferred_element_type=F32
    )
    term = jnp.dot(aggregated.T, delta, precision=highest, preferred_element_type=F32)
    for k in range(4):
        term_ref[at_ref[3] ^ k] = term[k * 64 : (k + 1) * 64]


def middle(at, own, other, weight, cotangent, panel):
    return pl.pallas_call(
        middle_kernel,
        in_specs=[pl.BlockSpec(memory_space=pltpu.SMEM)] + [IN_VMEM] * 6,
        out_shape=[
            jax.ShapeDtypeStruct((128, 256), F32),
            jax.ShapeDtypeStruct((4, 64, 256), F32),
            jax.ShapeDtypeStruct((256, 128), F32),
        ],
        compiler_params=pltpu.CompilerParams(vmem_limit_bytes=LIMIT),
        name="middle",
    )(at, own, other, weight, cotangent, *panel)


def assemble_kernel(scale, at_ref, near_ref, far_ref, out_ref):
    for k in range(4):
        place = at_ref[3] ^ k
        odd = (place & 1).astype(F32)
        i = place >> 1
        part = jnp.where(odd > 0.5, far_ref[i], near_ref[i])
        out_ref[k * 64 : (k + 1) * 64] = part * scale


def assemble(at, near, far, scale):
    return pl.pallas_call(
        functools.partial(assemble_kernel, scale),
        in_specs=[pl.BlockSpec(memory_space=pltpu.SMEM)] + [IN_VMEM] * 2,
        out_shape=jax.ShapeDtypeStruct((256, 256), F32),
        compiler_params=pltpu.CompilerParams(vmem_limit_bytes=LIMIT),
        name="assemble",
    )(at, near, far)


def backward_kernel(jobs, near_ref, far_ref, high, low, after, *outs):
    i = pl.program_id(0)
    backs = (near_ref.at[0], far_ref.at[0], near_ref.at[1], far_ref.at[1])
    for (half, pick), out in zip(jobs, outs):
        back = jnp.concatenate([ref[pl.ds(half * 128, 128), :] for ref in backs], axis=1)
        b_high, b_low = split(back)
        both = mm(jnp.concatenate([b_high, b_low], axis=0), wide(high, half, pick(i)))
        result = both[:128] + (both[128:] + mm(b_high, wide(low, half, pick(i))))
        for dz in range(SIDE):
            out[0, dz] = result[:, dz * 128 : (dz + 1) * 128]


def backward(panel, back, steps, jobs, after):
    return pl.pallas_call(
        functools.partial(backward_kernel, jobs),
        grid=(steps,),
        in_specs=[pl.BlockSpec((2, 256, 128), lambda i: (0, 0, 0))] * 2
        + [IN_VMEM, IN_VMEM, pl.BlockSpec(memory_space=pl.ANY)],
        out_specs=[pl.BlockSpec((1, SIDE, 128, 128), lambda i: (i, 0, 0, 0)) for _ in jobs],
        out_shape=[jax.ShapeDtypeStruct((steps, SIDE, 128, 128), F32) for _ in jobs],
        cost_estimate=pl.CostEstimate(
            flops=len(jobs) * steps * 4 * 2 * 512 * 512 * 128,
            bytes_accessed=len(jobs) * steps * 13 * 10**5,
            transcendentals=0,
        ),
        compiler_params=pltpu.CompilerParams(vmem_limit_bytes=LIMIT),
        name="backward",
    )(*back, *panel, after)


BIG = ("x", "y")
MID = ("y", "x")


def gather_forward(features, panel):
    two = jnp.stack([features[:, :128], features[:, 128:]])
    by_z = [two] + [send(two, "z", -d) for d in (1, 2, 3)]
    totals = [jnp.zeros((512, 128), F32)] * 2
    near = []
    for half in range(2):
        mine = jnp.stack([block[half] for block in by_z])
        near.append(jnp.stack([mine] + [send(mine, MID[half], -d) for d in (1, 2, 3)]))
    first = [(send(near[h], BIG[h], -1), send(near[h], BIG[h], 1)) for h in range(2)]
    totals = forward(panel, totals, 4, [(h, lambda i: (0, i), near[h]) for h in range(2)])
    second = [
        (send(first[h][0][:2], BIG[h], -1), send(first[h][1][2:], BIG[h], 1)) for h in range(2)
    ]
    totals = forward(
        panel,
        totals,
        4,
        [(h, lambda i, d=d: (d, i), first[h][j]) for h in range(2) for j, d in enumerate((1, 3))],
    )
    totals = forward(
        panel,
        totals,
        2,
        [(h, lambda i, j=j: (2, 2 * j + i), second[h][j]) for h in range(2) for j in range(2)],
    )
    return totals, panel


def scatter_backward(back, panel, pair):
    early = backward(
        panel,
        back,
        4,
        [
            (h, pick)
            for h in range(2)
            for pick in (
                lambda i: (1 + lax.div(i, 2), lax.rem(i + 2, 4)),
                lambda i: (3 - lax.div(i, 2), i),
            )
        ],
        pair,
    )
    late = backward(
        panel,
        back,
        2,
        [
            (h, pick)
            for h in range(2)
            for pick in (
                lambda i: (1, i),
                lambda i: (3, i + 2),
                lambda i: (0, i),
                lambda i: (0, i + 2),
            )
        ],
        pair,
    )
    ups = [send(early[2 * h], BIG[h], 1) for h in range(2)]
    downs = [send(early[2 * h + 1], BIG[h], -1) for h in range(2)]
    piece = pair[0] + swap(pair[1], 2)
    for mask in (1, 3):
        piece = piece + trade(piece, "z", mask)
    *relays, piece = relay(late, ups, downs, piece.reshape(128, 128))
    relays_up = [send(relays[2 * h], BIG[h], 1) for h in range(2)]
    relays_down = [send(relays[2 * h + 1], BIG[h], -1) for h in range(2)]
    parts = merge(late, ups, downs, relays_up, relays_down, piece)
    moved = [
        [parts[4 * h]] + [send(parts[4 * h + d], MID[h], d) for d in (1, 2, 3)] for h in range(2)
    ]
    *both, piece = settle(moved)
    moved = [both[0]] + [send(both[d], "z", d) for d in (1, 2, 3)]
    near, far = spread(piece.reshape(64, 256))
    return finish(moved), near, far


def relay_kernel(*refs):
    for late, come, out in zip(refs[:4], refs[4:8], refs[9:13]):
        out[...] = late[...] + come[...]
    refs[13][...] = refs[8][...]


def relay(late, ups, downs, piece):
    own = pl.BlockSpec((1, SIDE, 128, 128), lambda i: (i, 0, 0, 0))
    come = pl.BlockSpec((1, SIDE, 128, 128), lambda i: (i + 2, 0, 0, 0))
    tail = pl.BlockSpec((128, 128), lambda i: (0, 0))
    return pl.pallas_call(
        relay_kernel,
        grid=(2,),
        in_specs=[own] * 4 + [come] * 4 + [tail],
        out_specs=[own] * 4 + [tail],
        out_shape=[jax.ShapeDtypeStruct((2, SIDE, 128, 128), F32)] * 4
        + [jax.ShapeDtypeStruct((128, 128), F32)],
        cost_estimate=pl.CostEstimate(flops=10**6, bytes_accessed=6 * 10**6, transcendentals=0),
        compiler_params=pltpu.CompilerParams(vmem_limit_bytes=LIMIT),
        name="relay",
    )(late[0], late[1], late[4], late[5], ups[0], downs[0], ups[1], downs[1], piece)


def merge_kernel(*refs):
    piece, outs = refs[12], refs[13:]
    i = pl.program_id(0)

    @pl.when(i < SIDE)
    def _():
        for h in range(2):
            for j in range(2):
                own, come, relayed = refs[6 * h + 3 * j : 6 * h + 3 * j + 3]
                for o in range(2):
                    outs[4 * h + 2 * j + o][0] = own[o, 0] + come[o, 0] + relayed[o, 0]

    @pl.when(i == SIDE)
    def _():
        for out in outs[:4]:
            out[0] = piece[...]


def merge(late, ups, downs, relays_up, relays_down, piece):
    two = pl.BlockSpec((2, 1, 128, 128), lambda i: (0, lax.min(i, SIDE - 1), 0, 0))
    args = []
    for h in range(2):
        args += [late[4 * h + 2], downs[h], relays_up[h], late[4 * h + 3], ups[h], relays_down[h]]
    return pl.pallas_call(
        merge_kernel,
        grid=(SIDE + 1,),
        in_specs=[two] * 12 + [pl.BlockSpec((128, 128), lambda i: (0, 0))],
        out_specs=[pl.BlockSpec((1, 128, 128), lambda i: (i, 0, 0))] * 4
        + [pl.BlockSpec((1, 128, 128), lambda i: (lax.min(i, SIDE - 1), 0, 0))] * 4,
        out_shape=[jax.ShapeDtypeStruct((SIDE + 1, 128, 128), F32)] * 4
        + [jax.ShapeDtypeStruct((SIDE, 128, 128), F32)] * 4,
        cost_estimate=pl.CostEstimate(flops=10**6, bytes_accessed=8 * 10**6, transcendentals=0),
        compiler_params=pltpu.CompilerParams(vmem_limit_bytes=LIMIT),
        name="merge",
    )(*args, piece)


def settle_kernel(*refs):
    ins, both, piece = refs[:8], refs[8:12], refs[12]

    def summed(half, i):
        a, b, c, d = ins[4 * half : 4 * half + 4]
        return (a[i] + c[i]) + (b[i] + d[i])

    for half in range(2):
        for dz in range(SIDE):
            both[dz][half] = summed(half, dz)
    piece[...] = summed(0, SIDE)


def settle(moved):
    return pl.pallas_call(
        settle_kernel,
        in_specs=[IN_VMEM] * 8,
        out_specs=[IN_VMEM] * 5,
        out_shape=[jax.ShapeDtypeStruct((2, 128, 128), F32)] * 4
        + [jax.ShapeDtypeStruct((128, 128), F32)],
        cost_estimate=pl.CostEstimate(flops=10**6, bytes_accessed=3 * 10**6, transcendentals=0),
        compiler_params=pltpu.CompilerParams(vmem_limit_bytes=LIMIT),
        name="settle",
    )(*moved[0], *moved[1])


def finish_kernel(a, b, c, d, out):
    total = (a[...] + c[...]) + (b[...] + d[...])
    for half in range(2):
        out[:, half * 128 : (half + 1) * 128] = total[half].T


def finish(moved):
    return pl.pallas_call(
        finish_kernel,
        in_specs=[IN_VMEM] * 4,
        out_specs=IN_VMEM,
        out_shape=jax.ShapeDtypeStruct((128, 256), F32),
        compiler_params=pltpu.CompilerParams(vmem_limit_bytes=LIMIT),
        name="finish",
    )(*moved)


def collect(value):
    given = swap(jnp.stack([value[1], value[3]]), 1)
    return value[0] + given[0], swap(value[2] + given[1], 2)


def spread(value):
    near = jnp.stack([value, swap(value, 2)])
    return near, swap(near, 1)


def body(features, weight, cotangent, tiles, tile_count, tile_block):
    g, r = lax.axis_index("rows"), lax.axis_index("rep")
    at = jnp.stack([g // 16, (g // 4) % 4, g % 4, r]).astype(jnp.int32)
    panel = make_panel(at, tile_count.reshape(-1), tile_block.reshape(-1), tiles[0, 0])
    totals, panel = gather_forward(features, panel)
    own, other = collect(jnp.concatenate(totals, axis=1).reshape(4, 128, 256))
    hidden, term, back = middle(at, own, other, weight, cotangent, panel)
    given = swap(jnp.stack([term[1], term[3]]), 1)
    pair = jnp.stack([term[0] + given[0], term[2] + given[1]])
    pair = (pair + send(pair, "x", 2)) + (send(pair, "x", 1) + send(pair, "x", 3))
    grad_features, near, far = scatter_backward(spread(back), panel, pair)
    node_total = 128 * lax.axis_size("rows") * lax.axis_size("rep")
    return hidden, assemble(at, near, far, 1.0 / math.sqrt(node_total)), grad_features


def solution(mesh):
    in_specs = (
        P(("rows", "rep"), None),
        P(),
        P(("rows", "rep"), None),
        P("rows", "rep", None, None, None, None),
        P("rows", "rep", None),
        P("rows", "rep", None, None),
    )
    out_specs = (P(("rows", "rep"), None), P(), P(("rows", "rep"), None))
    return jax.shard_map(body, mesh=mesh, in_specs=in_specs, out_specs=out_specs, check_vma=False)
```

```python
import functools
import math

import jax
import jax.numpy as jnp
from jax import lax
from jax.experimental import pallas as pl
from jax.experimental.pallas import tpu as pltpu
from jax.sharding import PartitionSpec as P

SIDE = 4
F32 = jnp.float32
BF16 = jnp.bfloat16
LIMIT = 16 * 2**20


def row_index(x, z, y):
    return (x * SIDE + z) * SIDE + y


def toward(axis, step):
    pairs = []
    for x in range(SIDE):
        for z in range(SIDE):
            for y in range(SIDE):
                at = [x, z, y]
                at["xzy".index(axis)] = (at["xzy".index(axis)] + step) % SIDE
                pairs.append((row_index(x, z, y), row_index(*at)))
    return pairs


def send(value, axis, step):
    return lax.ppermute(value, "rows", toward(axis, step))


def trade(value, axis, mask):
    pairs = []
    for x in range(SIDE):
        for z in range(SIDE):
            for y in range(SIDE):
                at = [x, z, y]
                at["xzy".index(axis)] ^= mask
                pairs.append((row_index(x, z, y), row_index(*at)))
    return lax.ppermute(value, "rows", pairs)


def swap(value, bit):
    return lax.ppermute(value, "rep", [(r, r ^ bit) for r in range(4)])


def split(value):
    high = value.astype(BF16)
    return high, (value - high.astype(F32)).astype(BF16)


def mm(left, right):
    return jnp.dot(left, right, preferred_element_type=F32)


def panel_kernel(at_ref, count_ref, block_ref, tiles_ref, high_ref, low_ref):
    x = lax.rem(at_ref[0] + pl.program_id(0), SIDE)
    z = lax.rem(at_ref[1] + pl.program_id(1), SIDE)
    for dy in range(SIDE):
        y = lax.rem(at_ref[2] + dy, SIDE)
        section = row_index(x, z, y)
        count = count_ref[section]
        first, second = block_ref[2 * section], block_ref[2 * section + 1]
        for k in range(4):
            block = at_ref[3] ^ k
            w0 = jnp.where((first == block) & (count > 0), 1.0, 0.0).astype(F32)
            w1 = jnp.where((second == block) & (count > 1), 1.0, 0.0).astype(F32)
            high, low = split(tiles_ref[0, 0, y, 0] * w0 + tiles_ref[0, 0, y, 1] * w1)
            high_ref[0, dy, 0, pl.ds(k * 128, 128), :] = high
            low_ref[0, dy, 0, pl.ds(k * 128, 128), :] = low


def make_panel(at, counts, blocks, tiles):
    shape = jax.ShapeDtypeStruct((SIDE, SIDE, SIDE, 512, 128), BF16)
    out_spec = pl.BlockSpec((1, SIDE, 1, 512, 128), lambda i, j, at, c, b: (i, 0, j, 0, 0))
    return pl.pallas_call(
        panel_kernel,
        grid_spec=pltpu.PrefetchScalarGridSpec(
            num_scalar_prefetch=3,
            grid=(SIDE, SIDE),
            in_specs=[
                pl.BlockSpec(
                    (1, 1, SIDE, 2, 128, 128),
                    lambda i, j, at, c, b: (
                        lax.rem(at[0] + i, SIDE),
                        lax.rem(at[1] + j, SIDE),
                        0,
                        0,
                        0,
                        0,
                    ),
                )
            ],
            out_specs=[out_spec, out_spec],
        ),
        out_shape=[shape, shape],
        cost_estimate=pl.CostEstimate(flops=10**8, bytes_accessed=25 * 10**6, transcendentals=0),
        compiler_params=pltpu.CompilerParams(vmem_limit_bytes=LIMIT),
        name="panel",
    )(at, counts, blocks, tiles.reshape(SIDE, SIDE, SIDE, 2, 128, 128))


def wide(ref, half, place):
    d, o = place
    i, j = (d, o) if half == 0 else (o, d)
    return jnp.concatenate([ref[i, j, dz] for dz in range(SIDE)], axis=1)


IN_VMEM = pl.BlockSpec(memory_space=pltpu.VMEM)


def forward_kernel(jobs, high, low, *refs):
    n = len(jobs)
    blocks, starts, totals = refs[:n], refs[n : n + 2], refs[n + 2 :]
    i = pl.program_id(0)

    @pl.when(i == 0)
    def _():
        for start, total in zip(starts, totals):
            total[...] = start[...]

    for (half, pick), block in zip(jobs, blocks):
        g_high, g_low = split(block[0].reshape(SIDE * 128, 128))
        both = mm(wide(high, half, pick(i)), jnp.concatenate([g_high, g_low], axis=1))
        totals[half][...] += both[:, :128] + (both[:, 128:] + mm(wide(low, half, pick(i)), g_high))


def forward(panel, totals, steps, jobs):
    whole = pl.BlockSpec((512, 128), lambda i: (0, 0))
    return pl.pallas_call(
        functools.partial(forward_kernel, [job[:2] for job in jobs]),
        grid=(steps,),
        in_specs=[IN_VMEM, IN_VMEM]
        + [pl.BlockSpec((1, SIDE, 128, 128), lambda i: (i, 0, 0, 0)) for _ in jobs]
        + [whole, whole],
        out_specs=[whole, whole],
        out_shape=[jax.ShapeDtypeStruct((512, 128), F32)] * 2,
        cost_estimate=pl.CostEstimate(
            flops=len(jobs) * steps * 4 * 2 * 512 * 512 * 128,
            bytes_accessed=len(jobs) * steps * 13 * 10**5,
            transcendentals=0,
        ),
        compiler_params=pltpu.CompilerParams(vmem_limit_bytes=LIMIT),
        name="forward",
    )(*panel, *[array for _, _, array in jobs], *totals)


def middle_kernel(at_ref, own_ref, other_ref, weight_ref, cot_ref, high, low, hidden_ref, term_ref, back_ref):
    highest = lax.Precision.HIGHEST
    aggregated = own_ref[...] + other_ref[...]
    weight = weight_ref[...]
    pre = jnp.dot(aggregated, weight, precision=highest, preferred_element_type=F32)
    sig = 1.0 / (1.0 + jnp.exp(-pre))
    hidden_ref[...] = pre * sig
    delta = cot_ref[...] * (sig * (1.0 + pre * (1.0 - sig)))
    back_ref[...] = lax.dot_general(
        weight, delta, (((1,), (1,)), ((), ())), precision=highest, preferred_element_type=F32
    )
    term = jnp.dot(aggregated.T, delta, precision=highest, preferred_element_type=F32)
    for k in range(4):
        term_ref[at_ref[3] ^ k] = term[k * 64 : (k + 1) * 64]


def middle(at, own, other, weight, cotangent, panel):
    return pl.pallas_call(
        middle_kernel,
        in_specs=[pl.BlockSpec(memory_space=pltpu.SMEM)] + [IN_VMEM] * 6,
        out_shape=[
            jax.ShapeDtypeStruct((128, 256), F32),
            jax.ShapeDtypeStruct((4, 64, 256), F32),
            jax.ShapeDtypeStruct((256, 128), F32),
        ],
        compiler_params=pltpu.CompilerParams(vmem_limit_bytes=LIMIT),
        name="middle",
    )(at, own, other, weight, cotangent, *panel)


def assemble_kernel(scale, at_ref, near_ref, far_ref, out_ref):
    for k in range(4):
        place = at_ref[3] ^ k
        odd = (place & 1).astype(F32)
        i = place >> 1
        part = jnp.where(odd > 0.5, far_ref[i], near_ref[i])
        out_ref[k * 64 : (k + 1) * 64] = part * scale


def assemble(at, near, far, scale):
    return pl.pallas_call(
        functools.partial(assemble_kernel, scale),
        in_specs=[pl.BlockSpec(memory_space=pltpu.SMEM)] + [IN_VMEM] * 2,
        out_shape=jax.ShapeDtypeStruct((256, 256), F32),
        compiler_params=pltpu.CompilerParams(vmem_limit_bytes=LIMIT),
        name="assemble",
    )(at, near, far)


def backward_kernel(jobs, added, streamed, near_ref, far_ref, *refs):
    n = len(jobs)
    m = n if streamed else 1
    highs, lows, refs = refs[:m], refs[m : 2 * m], refs[2 * m :]
    i = pl.program_id(0)
    backs = (near_ref.at[0], far_ref.at[0], near_ref.at[1], far_ref.at[1])
    for at, (half, pick) in enumerate(jobs):
        out = refs[at - n]
        if streamed:
            a_high, a_low = wide(highs[at], 0, (0, 0)), wide(lows[at], 0, (0, 0))
        else:
            a_high, a_low = wide(highs[0], half, pick(i)), wide(lows[0], half, pick(i))
        back = jnp.concatenate([ref[pl.ds(half * 128, 128), :] for ref in backs], axis=1)
        b_high, b_low = split(back)
        both = mm(jnp.concatenate([b_high, b_low], axis=0), a_high)
        result = both[:128] + (both[128:] + mm(b_high, a_low))
        for dz in range(SIDE):
            term = result[:, dz * 128 : (dz + 1) * 128]
            out[0, dz] = term + refs[at][0, dz] if added else term


def panel_spec(half, pick):
    def index(i):
        d, o = pick(i)
        return (d, o, 0, 0, 0) if half == 0 else (o, d, 0, 0, 0)

    return pl.BlockSpec((1, 1, SIDE, 512, 128), index)


def backward(panel, back, steps, jobs, adds=(), after=()):
    block = (1, SIDE, 128, 128)
    streamed = bool(adds)
    specs = [panel_spec(half, pick) for half, pick in jobs] if streamed else [IN_VMEM]
    return pl.pallas_call(
        functools.partial(backward_kernel, jobs, bool(adds), streamed),
        grid=(steps,),
        in_specs=[pl.BlockSpec((2, 256, 128), lambda i: (0, 0, 0))] * 2
        + specs * 2
        + [pl.BlockSpec(block, lambda i, offset=offset: (i + offset, 0, 0, 0)) for _, offset in adds]
        + [pl.BlockSpec(memory_space=pl.ANY) for _ in after],
        out_specs=[pl.BlockSpec(block, lambda i: (i, 0, 0, 0)) for _ in jobs],
        out_shape=[jax.ShapeDtypeStruct((steps, SIDE, 128, 128), F32) for _ in jobs],
        cost_estimate=pl.CostEstimate(
            flops=len(jobs) * steps * 4 * 2 * 512 * 512 * 128,
            bytes_accessed=len(jobs) * steps * 13 * 10**5,
            transcendentals=0,
        ),
        compiler_params=pltpu.CompilerParams(vmem_limit_bytes=(50 if streamed else 16) * 2**20),
        name="backward",
    )(
        *back,
        *[panel[0]] * len(specs),
        *[panel[1]] * len(specs),
        *[array for array, _ in adds],
        *after,
    )


BIG = ("x", "y")
MID = ("y", "x")


def gather_forward(features, panel):
    two = jnp.stack([features[:, :128], features[:, 128:]])
    by_z = [two] + [send(two, "z", -d) for d in (1, 2, 3)]
    totals = [jnp.zeros((512, 128), F32)] * 2
    near = []
    for half in range(2):
        mine = jnp.stack([block[half] for block in by_z])
        near.append(jnp.stack([mine] + [send(mine, MID[half], -d) for d in (1, 2, 3)]))
    first = [(send(near[h], BIG[h], -1), send(near[h], BIG[h], 1)) for h in range(2)]
    totals = forward(panel, totals, 4, [(h, lambda i: (0, i), near[h]) for h in range(2)])
    second = [
        (send(first[h][0][:2], BIG[h], -1), send(first[h][1][2:], BIG[h], 1)) for h in range(2)
    ]
    totals = forward(
        panel,
        totals,
        4,
        [(h, lambda i, d=d: (d, i), first[h][j]) for h in range(2) for j, d in enumerate((1, 3))],
    )
    totals = forward(
        panel,
        totals,
        2,
        [(h, lambda i, j=j: (2, 2 * j + i), second[h][j]) for h in range(2) for j in range(2)],
    )
    return totals, panel


def scatter_backward(back, panel, pair):
    early = backward(
        panel,
        back,
        4,
        [
            (h, pick)
            for h in range(2)
            for pick in (
                lambda i: (1 + lax.div(i, 2), lax.rem(i + 2, 4)),
                lambda i: (3 - lax.div(i, 2), i),
            )
        ],
        after=[pair],
    )
    ups = [send(early[2 * h], BIG[h], 1) for h in range(2)]
    downs = [send(early[2 * h + 1], BIG[h], -1) for h in range(2)]
    piece = pair[0] + swap(pair[1], 2)
    for mask in (1, 3):
        piece = piece + trade(piece, "z", mask)
    piece = piece.reshape(128, 128)
    relays = backward(
        panel,
        back,
        2,
        [(h, pick) for h in range(2) for pick in (lambda i: (1, i), lambda i: (3, i + 2))],
        [(array, 2) for h in range(2) for array in (ups[h], downs[h])],
        [piece],
    )
    own = backward(
        panel,
        back,
        2,
        [(h, pick) for h in range(2) for pick in (lambda i: (0, i), lambda i: (0, i + 2))],
        [(array, 0) for h in range(2) for array in (downs[h], ups[h])],
        [relays[0]],
    )
    far = [send(relays[j], BIG[j // 2], 1 - 2 * (j % 2)) for j in range(4)]
    parts = merge(own, far, piece)
    moved = [
        [parts[4 * h]] + [send(parts[4 * h + d], MID[h], d) for d in (1, 2, 3)] for h in range(2)
    ]
    *both, piece = settle(moved)
    moved = [both[0]] + [send(both[d], "z", d) for d in (1, 2, 3)]
    near, far = spread(piece.reshape(64, 256))
    return finish(moved), near, far


def merge_kernel(*refs):
    owns, fars, piece, outs = refs[:4], refs[4:8], refs[8], refs[9:]
    i = pl.program_id(0)

    @pl.when(i < SIDE)
    def _():
        for j in range(4):
            for o in range(2):
                outs[2 * j + o][0] = owns[j][o, 0] + fars[j][o, 0]

    @pl.when(i == SIDE)
    def _():
        for out in outs[:4]:
            out[0] = piece[...]


def merge(own, far, piece):
    two = pl.BlockSpec((2, 1, 128, 128), lambda i: (0, lax.min(i, SIDE - 1), 0, 0))
    return pl.pallas_call(
        merge_kernel,
        grid=(SIDE + 1,),
        in_specs=[two] * 8 + [pl.BlockSpec((128, 128), lambda i: (0, 0))],
        out_specs=[pl.BlockSpec((1, 128, 128), lambda i: (i, 0, 0))] * 4
        + [pl.BlockSpec((1, 128, 128), lambda i: (lax.min(i, SIDE - 1), 0, 0))] * 4,
        out_shape=[jax.ShapeDtypeStruct((SIDE + 1, 128, 128), F32)] * 4
        + [jax.ShapeDtypeStruct((SIDE, 128, 128), F32)] * 4,
        cost_estimate=pl.CostEstimate(flops=10**6, bytes_accessed=6 * 10**6, transcendentals=0),
        compiler_params=pltpu.CompilerParams(vmem_limit_bytes=LIMIT),
        name="merge",
    )(*own, *far, piece)


def settle_kernel(*refs):
    ins, both, piece = refs[:8], refs[8:12], refs[12]

    def summed(half, i):
        a, b, c, d = ins[4 * half : 4 * half + 4]
        return (a[i] + c[i]) + (b[i] + d[i])

    for half in range(2):
        for dz in range(SIDE):
            both[dz][half] = summed(half, dz)
    piece[...] = summed(0, SIDE)


def settle(moved):
    return pl.pallas_call(
        settle_kernel,
        in_specs=[IN_VMEM] * 8,
        out_specs=[IN_VMEM] * 5,
        out_shape=[jax.ShapeDtypeStruct((2, 128, 128), F32)] * 4
        + [jax.ShapeDtypeStruct((128, 128), F32)],
        cost_estimate=pl.CostEstimate(flops=10**6, bytes_accessed=3 * 10**6, transcendentals=0),
        compiler_params=pltpu.CompilerParams(vmem_limit_bytes=LIMIT),
        name="settle",
    )(*moved[0], *moved[1])


def finish_kernel(a, b, c, d, out):
    total = (a[...] + c[...]) + (b[...] + d[...])
    for half in range(2):
        out[:, half * 128 : (half + 1) * 128] = total[half].T


def finish(moved):
    return pl.pallas_call(
        finish_kernel,
        in_specs=[IN_VMEM] * 4,
        out_specs=IN_VMEM,
        out_shape=jax.ShapeDtypeStruct((128, 256), F32),
        compiler_params=pltpu.CompilerParams(vmem_limit_bytes=LIMIT),
        name="finish",
    )(*moved)


def collect(value):
    given = swap(jnp.stack([value[1], value[3]]), 1)
    return value[0] + given[0], swap(value[2] + given[1], 2)


def spread(value):
    near = jnp.stack([value, swap(value, 2)])
    return near, swap(near, 1)


def body(features, weight, cotangent, tiles, tile_count, tile_block):
    g, r = lax.axis_index("rows"), lax.axis_index("rep")
    at = jnp.stack([g // 16, (g // 4) % 4, g % 4, r]).astype(jnp.int32)
    panel = make_panel(at, tile_count.reshape(-1), tile_block.reshape(-1), tiles[0, 0])
    totals, panel = gather_forward(features, panel)
    own, other = collect(jnp.concatenate(totals, axis=1).reshape(4, 128, 256))
    hidden, term, back = middle(at, own, other, weight, cotangent, panel)
    given = swap(jnp.stack([term[1], term[3]]), 1)
    pair = jnp.stack([term[0] + given[0], term[2] + given[1]])
    pair = (pair + send(pair, "x", 2)) + (send(pair, "x", 1) + send(pair, "x", 3))
    grad_features, near, far = scatter_backward(spread(back), panel, pair)
    node_total = 128 * lax.axis_size("rows") * lax.axis_size("rep")
    return hidden, assemble(at, near, far, 1.0 / math.sqrt(node_total)), grad_features


def solution(mesh):
    in_specs = (
        P(("rows", "rep"), None),
        P(),
        P(("rows", "rep"), None),
        P("rows", "rep", None, None, None, None),
        P("rows", "rep", None),
        P("rows", "rep", None, None),
    )
    out_specs = (P(("rows", "rep"), None), P(), P(("rows", "rep"), None))
    return jax.shard_map(body, mesh=mesh, in_specs=in_specs, out_specs=out_specs, check_vma=False)
```

```python
import functools
import math

import jax
import jax.numpy as jnp
from jax import lax
from jax.experimental import pallas as pl
from jax.experimental.pallas import tpu as pltpu
from jax.sharding import PartitionSpec as P

SIDE = 4
F32 = jnp.float32
BF16 = jnp.bfloat16
LIMIT = 16 * 2**20


def row_index(x, z, y):
    return (x * SIDE + z) * SIDE + y


def toward(axis, step):
    pairs = []
    for x in range(SIDE):
        for z in range(SIDE):
            for y in range(SIDE):
                at = [x, z, y]
                at["xzy".index(axis)] = (at["xzy".index(axis)] + step) % SIDE
                pairs.append((row_index(x, z, y), row_index(*at)))
    return pairs


def send(value, axis, step):
    return lax.ppermute(value, "rows", toward(axis, step))


def trade(value, axis, mask):
    pairs = []
    for x in range(SIDE):
        for z in range(SIDE):
            for y in range(SIDE):
                at = [x, z, y]
                at["xzy".index(axis)] ^= mask
                pairs.append((row_index(x, z, y), row_index(*at)))
    return lax.ppermute(value, "rows", pairs)


def swap(value, bit):
    return lax.ppermute(value, "rep", [(r, r ^ bit) for r in range(4)])


def split(value):
    high = value.astype(BF16)
    return high, (value - high.astype(F32)).astype(BF16)


def mm(left, right):
    return jnp.dot(left, right, preferred_element_type=F32)


def panel_kernel(at_ref, count_ref, block_ref, tiles_ref, high_ref, low_ref):
    x = lax.rem(at_ref[0] + pl.program_id(0), SIDE)
    z = lax.rem(at_ref[1] + pl.program_id(1), SIDE)
    for dy in range(SIDE):
        y = lax.rem(at_ref[2] + dy, SIDE)
        section = row_index(x, z, y)
        count = count_ref[section]
        first, second = block_ref[2 * section], block_ref[2 * section + 1]
        for k in range(4):
            block = at_ref[3] ^ k
            w0 = jnp.where((first == block) & (count > 0), 1.0, 0.0).astype(F32)
            w1 = jnp.where((second == block) & (count > 1), 1.0, 0.0).astype(F32)
            high, low = split(tiles_ref[0, 0, y, 0] * w0 + tiles_ref[0, 0, y, 1] * w1)
            high_ref[0, dy, 0, pl.ds(k * 128, 128), :] = high
            low_ref[0, dy, 0, pl.ds(k * 128, 128), :] = low


def make_panel(at, counts, blocks, tiles):
    shape = jax.ShapeDtypeStruct((SIDE, SIDE, SIDE, 512, 128), BF16)
    out_spec = pl.BlockSpec((1, SIDE, 1, 512, 128), lambda i, j, at, c, b: (i, 0, j, 0, 0))
    return pl.pallas_call(
        panel_kernel,
        grid_spec=pltpu.PrefetchScalarGridSpec(
            num_scalar_prefetch=3,
            grid=(SIDE, SIDE),
            in_specs=[
                pl.BlockSpec(
                    (1, 1, SIDE, 2, 128, 128),
                    lambda i, j, at, c, b: (
                        lax.rem(at[0] + i, SIDE),
                        lax.rem(at[1] + j, SIDE),
                        0,
                        0,
                        0,
                        0,
                    ),
                )
            ],
            out_specs=[out_spec, out_spec],
        ),
        out_shape=[shape, shape],
        cost_estimate=pl.CostEstimate(flops=10**8, bytes_accessed=25 * 10**6, transcendentals=0),
        compiler_params=pltpu.CompilerParams(vmem_limit_bytes=LIMIT),
        name="panel",
    )(at, counts, blocks, tiles.reshape(SIDE, SIDE, SIDE, 2, 128, 128))


def wide(ref, half, place, count=SIDE):
    d, o = place
    i, j = (d, o) if half == 0 else (o, d)
    return jnp.concatenate([ref[i, j, dz] for dz in range(count)], axis=1)


IN_VMEM = pl.BlockSpec(memory_space=pltpu.VMEM)


def forward_kernel(jobs, high, low, *refs):
    n = len(jobs)
    blocks, starts, totals = refs[:n], refs[n : n + 2], refs[n + 2 :]
    i = pl.program_id(0)

    @pl.when(i == 0)
    def _():
        for start, total in zip(starts, totals):
            total[...] = start[...]

    for (half, pick), block in zip(jobs, blocks):
        g_high, g_low = split(block[0].reshape(SIDE * 128, 128))
        both = mm(wide(high, half, pick(i)), jnp.concatenate([g_high, g_low], axis=1))
        totals[half][...] += both[:, :128] + (both[:, 128:] + mm(wide(low, half, pick(i)), g_high))


def forward(panel, totals, steps, jobs):
    whole = pl.BlockSpec((512, 128), lambda i: (0, 0))
    return pl.pallas_call(
        functools.partial(forward_kernel, [job[:2] for job in jobs]),
        grid=(steps,),
        in_specs=[IN_VMEM, IN_VMEM]
        + [pl.BlockSpec((1, SIDE, 128, 128), lambda i: (i, 0, 0, 0)) for _ in jobs]
        + [whole, whole],
        out_specs=[whole, whole],
        out_shape=[jax.ShapeDtypeStruct((512, 128), F32)] * 2,
        cost_estimate=pl.CostEstimate(
            flops=len(jobs) * steps * 4 * 2 * 512 * 512 * 128,
            bytes_accessed=len(jobs) * steps * 13 * 10**5,
            transcendentals=0,
        ),
        compiler_params=pltpu.CompilerParams(vmem_limit_bytes=LIMIT),
        name="forward",
    )(*panel, *[array for _, _, array in jobs], *totals)


def middle_kernel(at_ref, own_ref, other_ref, weight_ref, cot_ref, high, low, hidden_ref, term_ref, back_ref):
    highest = lax.Precision.HIGHEST
    aggregated = own_ref[...] + other_ref[...]
    weight = weight_ref[...]
    pre = jnp.dot(aggregated, weight, precision=highest, preferred_element_type=F32)
    sig = 1.0 / (1.0 + jnp.exp(-pre))
    hidden_ref[...] = pre * sig
    delta = cot_ref[...] * (sig * (1.0 + pre * (1.0 - sig)))
    back_ref[...] = lax.dot_general(
        weight, delta, (((1,), (1,)), ((), ())), precision=highest, preferred_element_type=F32
    )
    term = jnp.dot(aggregated.T, delta, precision=highest, preferred_element_type=F32)
    for k in range(4):
        term_ref[at_ref[3] ^ k] = term[k * 64 : (k + 1) * 64]


def middle(at, own, other, weight, cotangent, panel):
    return pl.pallas_call(
        middle_kernel,
        in_specs=[pl.BlockSpec(memory_space=pltpu.SMEM)] + [IN_VMEM] * 6,
        out_shape=[
            jax.ShapeDtypeStruct((128, 256), F32),
            jax.ShapeDtypeStruct((4, 64, 256), F32),
            jax.ShapeDtypeStruct((256, 128), F32),
        ],
        compiler_params=pltpu.CompilerParams(vmem_limit_bytes=LIMIT),
        name="middle",
    )(at, own, other, weight, cotangent, *panel)


def assemble_kernel(scale, at_ref, near_ref, far_ref, out_ref):
    for k in range(4):
        place = at_ref[3] ^ k
        odd = (place & 1).astype(F32)
        i = place >> 1
        part = jnp.where(odd > 0.5, far_ref[i], near_ref[i])
        out_ref[k * 64 : (k + 1) * 64] = part * scale


def assemble(at, near, far, scale):
    return pl.pallas_call(
        functools.partial(assemble_kernel, scale),
        in_specs=[pl.BlockSpec(memory_space=pltpu.SMEM)] + [IN_VMEM] * 2,
        out_shape=jax.ShapeDtypeStruct((256, 256), F32),
        compiler_params=pltpu.CompilerParams(vmem_limit_bytes=LIMIT),
        name="assemble",
    )(at, near, far)


def backward_kernel(jobs, added, streamed, near_ref, far_ref, *refs):
    n = len(jobs)
    m = n if streamed else 1
    highs, lows, refs = refs[:m], refs[m : 2 * m], refs[2 * m :]
    i = pl.program_id(0)
    backs = (near_ref.at[0], far_ref.at[0], near_ref.at[1], far_ref.at[1])
    for at, (half, pick) in enumerate(jobs):
        out = refs[at - n]
        if streamed:
            a_high, a_low = wide(highs[at], 0, (0, 0), 2), wide(lows[at], 0, (0, 0), 2)
        else:
            a_high, a_low = wide(highs[0], half, pick(i)), wide(lows[0], half, pick(i))
        back = jnp.concatenate([ref[pl.ds(half * 128, 128), :] for ref in backs], axis=1)
        b_high, b_low = split(back)
        both = mm(jnp.concatenate([b_high, b_low], axis=0), a_high)
        result = both[:128] + (both[128:] + mm(b_high, a_low))
        for dz in range(2 if streamed else SIDE):
            term = result[:, dz * 128 : (dz + 1) * 128]
            out[0, dz] = term + refs[at][0, dz] if added else term


def panel_spec(half, pick):
    def index(i):
        d, o = pick(lax.div(i, 2))
        z = lax.rem(i, 2)
        return (d, o, z, 0, 0) if half == 0 else (o, d, z, 0, 0)

    return pl.BlockSpec((1, 1, 2, 512, 128), index)


def backward(panel, back, steps, jobs, adds=(), after=()):
    streamed = bool(adds)
    block = (1, 2, 128, 128) if streamed else (1, SIDE, 128, 128)

    def place(i, offset=0):
        return (lax.div(i, 2) + offset, lax.rem(i, 2), 0, 0) if streamed else (i, 0, 0, 0)

    specs = [panel_spec(half, pick) for half, pick in jobs] if streamed else [IN_VMEM]
    return pl.pallas_call(
        functools.partial(backward_kernel, jobs, bool(adds), streamed),
        grid=(2 * steps if streamed else steps,),
        in_specs=[pl.BlockSpec((2, 256, 128), lambda i: (0, 0, 0))] * 2
        + specs * 2
        + [pl.BlockSpec(block, functools.partial(place, offset=offset)) for _, offset in adds]
        + [pl.BlockSpec(memory_space=pl.ANY) for _ in after],
        out_specs=[pl.BlockSpec(block, place) for _ in jobs],
        out_shape=[jax.ShapeDtypeStruct((steps, SIDE, 128, 128), F32) for _ in jobs],
        cost_estimate=pl.CostEstimate(
            flops=len(jobs) * steps * 4 * 2 * 512 * 512 * 128,
            bytes_accessed=len(jobs) * steps * 13 * 10**5,
            transcendentals=0,
        ),
        compiler_params=pltpu.CompilerParams(vmem_limit_bytes=(50 if streamed else 16) * 2**20),
        name="backward",
    )(
        *back,
        *[panel[0]] * len(specs),
        *[panel[1]] * len(specs),
        *[array for array, _ in adds],
        *after,
    )


BIG = ("x", "y")
MID = ("y", "x")


def gather_forward(features, panel):
    two = jnp.stack([features[:, :128], features[:, 128:]])
    by_z = [two] + [send(two, "z", -d) for d in (1, 2, 3)]
    totals = [jnp.zeros((512, 128), F32)] * 2
    near = []
    for half in range(2):
        mine = jnp.stack([block[half] for block in by_z])
        near.append(jnp.stack([mine] + [send(mine, MID[half], -d) for d in (1, 2, 3)]))
    first = [(send(near[h], BIG[h], -1), send(near[h], BIG[h], 1)) for h in range(2)]
    totals = forward(panel, totals, 4, [(h, lambda i: (0, i), near[h]) for h in range(2)])
    second = [
        (send(first[h][0][:2], BIG[h], -1), send(first[h][1][2:], BIG[h], 1)) for h in range(2)
    ]
    totals = forward(
        panel,
        totals,
        4,
        [(h, lambda i, d=d: (d, i), first[h][j]) for h in range(2) for j, d in enumerate((1, 3))],
    )
    totals = forward(
        panel,
        totals,
        2,
        [(h, lambda i, j=j: (2, 2 * j + i), second[h][j]) for h in range(2) for j in range(2)],
    )
    return totals, panel


def scatter_backward(back, panel, pair):
    early = backward(
        panel,
        back,
        4,
        [
            (h, pick)
            for h in range(2)
            for pick in (
                lambda i: (1 + lax.div(i, 2), lax.rem(i + 2, 4)),
                lambda i: (3 - lax.div(i, 2), i),
            )
        ],
        after=[pair],
    )
    ups = [send(early[2 * h], BIG[h], 1) for h in range(2)]
    downs = [send(early[2 * h + 1], BIG[h], -1) for h in range(2)]
    piece = pair[0] + swap(pair[1], 2)
    for mask in (1, 3):
        piece = piece + trade(piece, "z", mask)
    piece = piece.reshape(128, 128)
    relays = backward(
        panel,
        back,
        2,
        [(h, pick) for h in range(2) for pick in (lambda i: (1, i), lambda i: (3, i + 2))],
        [(array, 2) for h in range(2) for array in (ups[h], downs[h])],
        [piece],
    )
    own = backward(
        panel,
        back,
        2,
        [(h, pick) for h in range(2) for pick in (lambda i: (0, i), lambda i: (0, i + 2))],
        [(array, 0) for h in range(2) for array in (downs[h], ups[h])],
        [relays[0]],
    )
    far = [send(relays[j], BIG[j // 2], 1 - 2 * (j % 2)) for j in range(4)]
    parts = merge(own, far, piece)
    moved = [
        [parts[4 * h]] + [send(parts[4 * h + d], MID[h], d) for d in (1, 2, 3)] for h in range(2)
    ]
    *both, piece = settle(moved)
    moved = [both[0]] + [send(both[d], "z", d) for d in (1, 2, 3)]
    near, far = spread(piece.reshape(64, 256))
    return finish(moved), near, far


def merge_kernel(*refs):
    owns, fars, piece, outs = refs[:4], refs[4:8], refs[8], refs[9:]
    i = pl.program_id(0)

    @pl.when(i < SIDE)
    def _():
        for j in range(4):
            for o in range(2):
                outs[2 * j + o][0] = owns[j][o, 0] + fars[j][o, 0]

    @pl.when(i == SIDE)
    def _():
        for out in outs[:4]:
            out[0] = piece[...]


def merge(own, far, piece):
    two = pl.BlockSpec((2, 1, 128, 128), lambda i: (0, lax.min(i, SIDE - 1), 0, 0))
    return pl.pallas_call(
        merge_kernel,
        grid=(SIDE + 1,),
        in_specs=[two] * 8 + [pl.BlockSpec((128, 128), lambda i: (0, 0))],
        out_specs=[pl.BlockSpec((1, 128, 128), lambda i: (i, 0, 0))] * 4
        + [pl.BlockSpec((1, 128, 128), lambda i: (lax.min(i, SIDE - 1), 0, 0))] * 4,
        out_shape=[jax.ShapeDtypeStruct((SIDE + 1, 128, 128), F32)] * 4
        + [jax.ShapeDtypeStruct((SIDE, 128, 128), F32)] * 4,
        cost_estimate=pl.CostEstimate(flops=10**6, bytes_accessed=6 * 10**6, transcendentals=0),
        compiler_params=pltpu.CompilerParams(vmem_limit_bytes=LIMIT),
        name="merge",
    )(*own, *far, piece)


def settle_kernel(*refs):
    ins, both, piece = refs[:8], refs[8:12], refs[12]

    def summed(half, i):
        a, b, c, d = ins[4 * half : 4 * half + 4]
        return (a[i] + c[i]) + (b[i] + d[i])

    for half in range(2):
        for dz in range(SIDE):
            both[dz][half] = summed(half, dz)
    piece[...] = summed(0, SIDE)


def settle(moved):
    return pl.pallas_call(
        settle_kernel,
        in_specs=[IN_VMEM] * 8,
        out_specs=[IN_VMEM] * 5,
        out_shape=[jax.ShapeDtypeStruct((2, 128, 128), F32)] * 4
        + [jax.ShapeDtypeStruct((128, 128), F32)],
        cost_estimate=pl.CostEstimate(flops=10**6, bytes_accessed=3 * 10**6, transcendentals=0),
        compiler_params=pltpu.CompilerParams(vmem_limit_bytes=LIMIT),
        name="settle",
    )(*moved[0], *moved[1])


def finish_kernel(a, b, c, d, out):
    total = (a[...] + c[...]) + (b[...] + d[...])
    for half in range(2):
        out[:, half * 128 : (half + 1) * 128] = total[half].T


def finish(moved):
    return pl.pallas_call(
        finish_kernel,
        in_specs=[IN_VMEM] * 4,
        out_specs=IN_VMEM,
        out_shape=jax.ShapeDtypeStruct((128, 256), F32),
        compiler_params=pltpu.CompilerParams(vmem_limit_bytes=LIMIT),
        name="finish",
    )(*moved)


def collect(value):
    given = swap(jnp.stack([value[1], value[3]]), 1)
    return value[0] + given[0], swap(value[2] + given[1], 2)


def spread(value):
    near = jnp.stack([value, swap(value, 2)])
    return near, swap(near, 1)


def body(features, weight, cotangent, tiles, tile_count, tile_block):
    g, r = lax.axis_index("rows"), lax.axis_index("rep")
    at = jnp.stack([g // 16, (g // 4) % 4, g % 4, r]).astype(jnp.int32)
    panel = make_panel(at, tile_count.reshape(-1), tile_block.reshape(-1), tiles[0, 0])
    totals, panel = gather_forward(features, panel)
    own, other = collect(jnp.concatenate(totals, axis=1).reshape(4, 128, 256))
    hidden, term, back = middle(at, own, other, weight, cotangent, panel)
    given = swap(jnp.stack([term[1], term[3]]), 1)
    pair = jnp.stack([term[0] + given[0], term[2] + given[1]])
    pair = (pair + send(pair, "x", 2)) + (send(pair, "x", 1) + send(pair, "x", 3))
    grad_features, near, far = scatter_backward(spread(back), panel, pair)
    node_total = 128 * lax.axis_size("rows") * lax.axis_size("rep")
    return hidden, assemble(at, near, far, 1.0 / math.sqrt(node_total)), grad_features


def solution(mesh):
    in_specs = (
        P(("rows", "rep"), None),
        P(),
        P(("rows", "rep"), None),
        P("rows", "rep", None, None, None, None),
        P("rows", "rep", None),
        P("rows", "rep", None, None),
    )
    out_specs = (P(("rows", "rep"), None), P(), P(("rows", "rep"), None))
    return jax.shard_map(body, mesh=mesh, in_specs=in_specs, out_specs=out_specs, check_vma=False)
```
